32 devices in a mesh: shard: 4 (over y, x), replica: 8 (over z, core).
Axes of the slice: x: 2, y: 2, z: 4, core: 2. Of those that a mesh axis runs over, the one named last changes fastest.
Arguments:
- tokens: bfloat16 [6304, 768], P(('shard', 'replica')), may hold values from -6 to 6
- ln_gain: bfloat16 [2, 2, 768], P(None, None, 'shard'), may hold values from 0.25 to 1.75
- ln_bias: bfloat16 [2, 2, 768], P(None, None, 'shard'), may hold values from -1.796875 to 1.796875
- w_qkv: bfloat16 [2, 768, 2304], P(None, 'shard'), may hold values from -0.21875 to 0.21875
- w_proj: bfloat16 [2, 768, 768], P(None, 'shard'), may hold values from -1.5 to 1.5
- w_router: bfloat16 [2, 768, 3], P(None, 'shard'), may hold values from -0.21875 to 0.21875
- expert_in: bfloat16 [2, 3, 3072, 768], P(None, None, 'shard'), may hold values from -0.21875 to 0.21875
- expert_out: bfloat16 [2, 3, 3072, 768], P(None, None, 'shard'), may hold values from -0.21875 to 0.21875
- image_count: int32 [32], P(('shard', 'replica')), may hold values from 0 to 1, as said below
- expert_ids: int32 [2, 6304, 2], P(None, ('shard', 'replica')), may hold values from 0 to 2, as said below
- slot_index: int32 [2, 6304, 2], P(None, ('shard', 'replica')), may hold values from -1 to 130, as said below
- cotangent: bfloat16 [6304, 768], P(('shard', 'replica')), may hold values from -6 to 6
Outputs:
- mixed: bfloat16 [6304, 768], P(('shard', 'replica'))
- grad_tokens: float32 [6304, 768], P(('shard', 'replica'))
- grad_gain: float32 [2, 2, 768], P(None, None, 'shard')
- grad_bias: float32 [2, 768], P(None, 'shard')
- grad_bias_second: float32 [2, 768], P(None, 'shard')
- grad_qkv: float32 [2, 768, 2304], P(None, 'shard')
- grad_proj: float32 [2, 768, 768], P(None, 'shard')
- grad_router: float32 [2, 768, 3], P(None, 'shard')
- grad_expert_in: float32 [2, 3, 3072, 768], P(None, None, 'shard')
- grad_expert_out: float32 [2, 3, 3072, 768], P(None, None, 'shard')
The draws below stay inside these ranges and needn't reach their ends.
Inputs may be any that keep to these rules, and one draw needn't show every extreme that they name: `image_count`: images present on a device fill its first image slots; some device has all 1 present. `expert_ids`: the two experts of a token differ. `slot_index`: on one device and in one block the positions taken in an expert's buffer are distinct and run from 0 up without gaps; -1 marks a dropped choice, and both choices of every row of an absent image are -1.
All inputs are finite; a program needn't handle non-finite values.
Results may differ from the reference program's by a relative error of at most 0.018.
Values may be sent and summed in bfloat16 or wider, within the bound.
A program may use at most 256 MiB of HBM per device.

```python
import jax
import jax.numpy as jnp
from jax import lax

D = 768
HEADS = 12
HEAD_DIM = 64
FF = 3072
SEQ = 197
EXPERTS = 3
LAYERS = 2
IMG_DEV = 1
ROWS = 197
CAP = 131
TOKENS = 6304
N_SHARD = 4
N_REPLICA = 8


def routing_tables(key):
    devices = N_SHARD * N_REPLICA
    keys = jax.random.split(key, 6)
    losses = jax.random.randint(keys[0], (devices,), 0, IMG_DEV + 1)
    struck = jax.random.randint(keys[1], (devices,), 0, 4) == 0
    counts = IMG_DEV - jnp.where(struck, losses, 0)
    full_device = jax.random.randint(keys[2], (), 0, devices)
    counts = jnp.where(jnp.arange(devices, dtype=jnp.int32) == full_device, IMG_DEV, counts).astype(jnp.int32)
    first = jax.random.randint(keys[3], (LAYERS, devices, ROWS), 0, EXPERTS)
    stride = jax.random.randint(keys[4], (LAYERS, devices, ROWS), 1, EXPERTS)
    second = (first + stride) % EXPERTS
    chosen = jnp.stack([first, second], axis=-1).astype(jnp.int32)
    priority = jax.random.randint(keys[5], (LAYERS, devices, ROWS), 0, 65536) * ROWS + jnp.arange(ROWS, dtype=jnp.int32)
    order = jnp.argsort(priority, axis=-1)
    ranking = jnp.argsort(order, axis=-1)
    present = jnp.arange(ROWS, dtype=jnp.int32)[None, :] // SEQ < counts[:, None]
    present = jnp.broadcast_to(present, (LAYERS, devices, ROWS))
    sorted_ids = jnp.take_along_axis(chosen, order[..., None], axis=2)
    sorted_live = jnp.take_along_axis(present, order, axis=2)
    queue = jnp.swapaxes(sorted_ids, 2, 3).reshape(LAYERS, devices, 2 * ROWS)
    queue_live = jnp.concatenate([sorted_live, sorted_live], axis=2)
    marks = ((queue[..., None] == jnp.arange(EXPERTS, dtype=jnp.int32)) & queue_live[..., None]).astype(jnp.int32)
    earlier = jnp.cumsum(marks, axis=2) - marks
    position = jnp.sum(earlier * marks, axis=-1)
    position = jnp.where(queue_live & (position < CAP), position, -1)
    position = jnp.swapaxes(position.reshape(LAYERS, devices, 2, ROWS), 2, 3)
    slots = jnp.take_along_axis(position, ranking[..., None], axis=2)
    return (counts, chosen.reshape(LAYERS, devices * ROWS, 2), slots.reshape(LAYERS, devices * ROWS, 2).astype(jnp.int32))


def draw_image_count(key, part):
    tables = routing_tables(key)
    return tables[0]


def draw_expert_ids(key, part):
    tables = routing_tables(key)
    return tables[1]


def draw_slot_index(key, part):
    tables = routing_tables(key)
    return tables[2]


def steps_of(own_key, dims, cuts, smallest, top_value):
    def one(dim, parts):
        heights = jax.random.uniform(jax.random.fold_in(jax.random.fold_in(own_key, 6), dim), (parts,), jnp.float32, smallest / len(cuts), top_value / len(cuts))
        return jnp.repeat(jnp.exp(heights), dims[dim] // parts).reshape((-1,) + (1,) * (len(dims) - dim - 1))

    loudness = one(*cuts[0])
    for cut in cuts[1:]:
        loudness = loudness * one(*cut)
    return loudness


def bell_draw(rng, extent, width, limit, shards=(), kind=jnp.bfloat16):
    array = width * jax.random.normal(rng, extent, jnp.float32)
    if shards:
        array = array * steps_of(rng, extent, shards, -0.22, 0.18)
    return jnp.clip(array, -limit, limit).astype(kind)


def setup_inputs(seed: int = 0) -> dict:
    splits = jax.random.split(jax.random.key(seed), 13)
    tokens = bell_draw(splits[0], (TOKENS, D), 1.0, 6.0, ((0, 32),))
    ln_gain = jnp.clip(1.0 + 0.15 * jax.random.normal(splits[1], (LAYERS, 2, D), jnp.float32), 0.25, 1.75).astype(jnp.bfloat16)
    ln_bias = bell_draw(splits[2], (LAYERS, 2, D), 0.3, 1.796875, ((2, 4),))
    w_qkv = bell_draw(splits[3], (LAYERS, D, 3 * D), D ** -0.5, 0.21875, ((1, 4),))
    w_proj = bell_draw(splits[4], (LAYERS, D, D), (D // 48) ** -0.5, 1.5, ((1, 4),))
    w_router = bell_draw(splits[5], (LAYERS, D, EXPERTS), D ** -0.5, 0.21875, ((1, 4),))
    expert_in = bell_draw(splits[6], (LAYERS, EXPERTS, FF, D), D ** -0.5, 0.21875, ((2, 4),))
    expert_out = bell_draw(splits[7], (LAYERS, EXPERTS, FF, D), (FF // 4) ** -0.5, 0.21875, ((2, 4),))
    image_count = draw_image_count(jax.random.fold_in(splits[12], 71), 0)
    expert_ids = draw_expert_ids(jax.random.fold_in(splits[12], 71), 0)
    slot_index = draw_slot_index(jax.random.fold_in(splits[12], 71), 0)
    cotangent = bell_draw(splits[11], (TOKENS, D), 1.0, 6.0, ((0, 32),))
    return {"tokens": tokens, "ln_gain": ln_gain, "ln_bias": ln_bias, "w_qkv": w_qkv, "w_proj": w_proj, "w_router": w_router, "expert_in": expert_in, "expert_out": expert_out, "image_count": image_count, "expert_ids": expert_ids, "slot_index": slot_index, "cotangent": cotangent}


precise = lax.Precision.HIGHEST

@jax.custom_vjp
def low(v):
    return lax.optimization_barrier(v.astype(jnp.bfloat16)).astype(jnp.float32)

@jax.custom_vjp
def low_back(v):
    return v

def low_keep(v):
    return (low(v), None)

def low_pass(kept, grad):
    return (grad,)

def back_keep(v):
    return (v, None)

def back_low(kept, grad):
    return (low(grad),)
low.defvjp(low_keep, low_pass)
low_back.defvjp(back_keep, back_low)

def layer_norm(values, gain, bias):
    centre = values - lax.optimization_barrier(jnp.mean(values, axis=-1, keepdims=True))
    spread = lax.optimization_barrier(jnp.mean(centre * centre, axis=-1, keepdims=True))
    return centre * lax.rsqrt(spread + 1e-06) * gain + bias

def attention(packed):
    blocks = packed.reshape(IMG_DEV, SEQ, 3, HEADS, HEAD_DIM)
    queries = blocks[:, :, 0]
    key_rows = blocks[:, :, 1]
    val_rows = blocks[:, :, 2]
    scores = low_back(jnp.einsum('bqhd,bkhd->bhqk', queries, key_rows, precision=precise) * 0.125)
    weights = low(jax.nn.softmax(scores, axis=-1))
    result = jnp.einsum('bhqk,bkhd->bqhd', weights, val_rows, precision=precise)
    return result.reshape(IMG_DEV * SEQ, D)

def block_layer(state, params, layer_idx, route_ids, route_slots):
    gains, biases, qkv_all, proj_all, router_all, in_all, out_all = params
    first = low(layer_norm(state, gains[layer_idx, 0], biases[layer_idx, 0]))
    packed = low_back(low(jnp.dot(first, qkv_all[layer_idx], precision=precise)))
    attended = low_back(low(attention(packed)))
    after = state + low_back(jnp.dot(attended, proj_all[layer_idx], precision=precise))
    second = low(layer_norm(after, gains[layer_idx, 1], biases[layer_idx, 1]))
    logits = jnp.dot(second, router_all[layer_idx], precision=precise)
    probs = jax.nn.softmax(logits, axis=-1)
    valid = route_slots >= 0
    flat_index = (route_ids * CAP + jnp.where(valid, route_slots, 0)).astype(jnp.int32)
    positions = jnp.arange(EXPERTS * CAP, dtype=jnp.int32)
    chosen = (flat_index[:, :, None] == positions[None, None, :]) & valid[:, :, None]
    table = lax.optimization_barrier(jnp.sum(chosen.astype(jnp.float32), axis=1))
    dispatched = jnp.dot(table.T, second, precision=precise).reshape(EXPERTS, CAP, D)
    before = low_back(jnp.einsum('ecd,efd->ecf', dispatched, in_all[layer_idx], precision=precise))
    hidden = low(jax.nn.gelu(before, approximate=False))
    returned = low_back(jnp.einsum('ecf,efd->ecd', hidden, out_all[layer_idx], precision=precise))
    returned = returned.reshape(EXPERTS * CAP, D)
    gates = jnp.take_along_axis(probs, route_ids, axis=1) * valid.astype(jnp.float32)
    picked = returned[flat_index]
    return after + lax.optimization_barrier(jnp.sum(gates[:, :, None] * picked, axis=1))

def device_block(state, live_rows, params, route_ids, route_slots):
    for layer_idx in range(LAYERS):
        state = block_layer(state, params, layer_idx, route_ids[layer_idx], route_slots[layer_idx])
    return state * live_rows[:, None]

def reference(tokens, ln_gain, ln_bias, w_qkv, w_proj, w_router, expert_in, expert_out, image_count, expert_ids, slot_index, cotangent):
    params = (ln_gain.astype(jnp.float32), ln_bias.astype(jnp.float32), w_qkv.astype(jnp.float32), w_proj.astype(jnp.float32), w_router.astype(jnp.float32), expert_in.astype(jnp.float32), expert_out.astype(jnp.float32))
    devices = image_count.shape[0]
    states = tokens.astype(jnp.float32).reshape(devices, ROWS, D)
    image_slot = jnp.arange(ROWS, dtype=jnp.int32) // SEQ
    live = (image_slot[None, :] < image_count[:, None]).astype(jnp.float32)
    route_ids = jnp.transpose(expert_ids.reshape(LAYERS, devices, ROWS, 2), (1, 0, 2, 3))
    route_slots = jnp.transpose(slot_index.reshape(LAYERS, devices, ROWS, 2), (1, 0, 2, 3))

    def forward(states_in, params_in):

        def one_device(carry, items):
            result = jax.checkpoint(device_block)(items[0], items[1], params_in, items[2], items[3])
            return (carry, result)
        _, outputs = lax.scan(one_device, jnp.zeros((), jnp.float32), (states_in, live, route_ids, route_slots))
        return outputs
    outputs, pullback = jax.vjp(forward, states, params)
    grad_states, grad_params = pullback(cotangent.astype(jnp.float32).reshape(devices, ROWS, D))
    return (outputs.reshape(devices * ROWS, D).astype(jnp.bfloat16), grad_states.reshape(devices * ROWS, D), grad_params[0], grad_params[1][:, 0], grad_params[1][:, 1], grad_params[2], grad_params[3], grad_params[4], grad_params[5], grad_params[6])
```

```python
import functools

import jax
import jax.numpy as jnp
from jax import lax
from jax.experimental import pallas as pl
from jax.experimental.pallas import tpu as pltpu
from jax.sharding import PartitionSpec as P

HEADS = 12
HEAD_DIM = 64
SEQ = 197
LANES = 128
MESH = pl.DeviceIdType.MESH

precise = lax.Precision.HIGHEST
VMEM = pl.BlockSpec(memory_space=pltpu.VMEM)


def round_up(value, step):
    return (value + step - 1) // step * step


def greet(devices):
    barrier = pltpu.get_barrier_semaphore()
    for device in devices:
        pl.semaphore_signal(barrier, inc=1, device_id=device, device_id_type=MESH)
    pl.semaphore_wait(barrier, len(devices))


def group_peers(n):
    me = lax.axis_index("shard")
    rep = lax.axis_index("replica")
    return me, [(lax.rem(me + k, n), rep) for k in range(1, n)]


def gather_kernel(n, x_ref, o_ref, send, recv):
    me, peers = group_peers(n)
    greet(peers)
    copies = []
    for k, peer in enumerate(peers):
        copy = pltpu.make_async_remote_copy(
            src_ref=x_ref,
            dst_ref=o_ref.at[me],
            send_sem=send.at[k],
            recv_sem=recv.at[k],
            device_id=peer,
            device_id_type=MESH,
        )
        copy.start()
        copies.append(copy)
    o_ref[me] = x_ref[...]
    for copy in copies:
        copy.wait()


def gather_rows(n, rows):
    return pl.pallas_call(
        functools.partial(gather_kernel, n),
        out_shape=jax.ShapeDtypeStruct((n,) + rows.shape, rows.dtype),
        in_specs=[VMEM],
        out_specs=VMEM,
        scratch_shapes=[pltpu.SemaphoreType.DMA((n - 1,)), pltpu.SemaphoreType.DMA((n - 1,))],
        compiler_params=pltpu.CompilerParams(collective_id=0, has_side_effects=True),
        name="gather_rows",
    )(rows)


def scatter_kernel(n, count, *refs):
    parts = refs[:count]
    outs = refs[count : 2 * count]
    lands = refs[2 * count : 3 * count]
    send, recv = refs[3 * count :]
    me, peers = group_peers(n)
    greet(peers)
    copies = []
    for k, peer in enumerate(peers):
        for i in range(count):
            copy = pltpu.make_async_remote_copy(
                src_ref=parts[i].at[peer[0]],
                dst_ref=lands[i].at[k],
                send_sem=send.at[i, k],
                recv_sem=recv.at[i, k],
                device_id=peer,
                device_id_type=MESH,
            )
            copy.start()
            copies.append(copy)
    for copy in copies:
        copy.wait()
    for i in range(count):
        total = parts[i][me].astype(jnp.float32)
        for k in range(n - 1):
            total = total + lands[i][k].astype(jnp.float32)
        outs[i][...] = total


def scatter_rows(n, parts, call_id):
    count = len(parts)
    return pl.pallas_call(
        functools.partial(scatter_kernel, n, count),
        out_shape=[jax.ShapeDtypeStruct(part.shape[1:], jnp.float32) for part in parts],
        in_specs=[VMEM] * count,
        out_specs=[VMEM] * count,
        scratch_shapes=[pltpu.VMEM((n - 1,) + part.shape[1:], part.dtype) for part in parts]
        + [pltpu.SemaphoreType.DMA((count, n - 1)), pltpu.SemaphoreType.DMA((count, n - 1))],
        compiler_params=pltpu.CompilerParams(collective_id=call_id, has_side_effects=True),
        name="scatter_rows",
    )(*parts)


def weights_kernel(n, halved, whole, *refs):
    count = halved + whole
    ins = refs[:count]
    outs = refs[count : 2 * count]
    send, recv, pass_send, pass_recv = refs[2 * count :]
    me, peers = group_peers(n)
    rep = lax.axis_index("replica")
    core = lax.rem(rep, 2)
    sibling = (me, rep + 1 - 2 * core)
    greet(peers + [sibling])
    copies = [[] for _ in range(count)]
    for i in list(range(halved, count)) + list(range(halved)):
        for k, peer in enumerate(peers):
            if i < halved:
                source, target = ins[i].at[core], outs[i].at[me, core]
            else:
                source, target = ins[i], outs[i].at[me]
            copy = pltpu.make_async_remote_copy(
                src_ref=source,
                dst_ref=target,
                send_sem=send.at[i, k],
                recv_sem=recv.at[i, k],
                device_id=peer,
                device_id_type=MESH,
            )
            copy.start()
            copies[i].append(copy)
    for i in range(count):
        outs[i][me] = ins[i][...]
    passed = []
    for i in range(halved):
        for k in range(n - 1):
            copies[i][k].wait_recv()
            owner = lax.rem(me + n - 1 - k, n)
            copy = pltpu.make_async_remote_copy(
                src_ref=outs[i].at[owner, core],
                dst_ref=outs[i].at[owner, core],
                send_sem=pass_send.at[i, k],
                recv_sem=pass_recv.at[i, k],
                device_id=sibling,
                device_id_type=MESH,
            )
            copy.start()
            passed.append(copy)
    for i in range(halved, count):
        for copy in copies[i]:
            copy.wait_recv()
    for i in range(count):
        for copy in copies[i]:
            copy.wait_send()
    for copy in passed:
        copy.wait()


def gather_weights(n, halved, whole):
    arrays = [a.reshape(2, a.shape[0] // 2, a.shape[1]) for a in halved] + list(whole)
    count = len(arrays)
    outs = pl.pallas_call(
        functools.partial(weights_kernel, n, len(halved), len(whole)),
        out_shape=[jax.ShapeDtypeStruct((n,) + a.shape, a.dtype) for a in arrays],
        in_specs=[VMEM] * count,
        out_specs=[VMEM] * count,
        scratch_shapes=[
            pltpu.SemaphoreType.DMA((count, n - 1)),
            pltpu.SemaphoreType.DMA((count, n - 1)),
            pltpu.SemaphoreType.DMA((len(halved), n - 1)),
            pltpu.SemaphoreType.DMA((len(halved), n - 1)),
        ],
        compiler_params=pltpu.CompilerParams(collective_id=3, has_side_effects=True),
        name="gather_weights",
    )(*arrays)
    full = [o.reshape(n * a.shape[0], a.shape[1]) for o, a in zip(outs, halved)]
    return full, outs[len(halved) :]


def norm_forward(values, gain, bias):
    centre = values - jnp.mean(values, axis=-1, keepdims=True)
    spread = jnp.mean(centre * centre, axis=-1, keepdims=True)
    scaled = lax.rsqrt(spread + 1e-06)
    normal = centre * scaled
    return (normal * gain + bias, normal, scaled)


def norm_backward(upstream, gain, normal, scaled):
    inner = upstream * gain
    centred = inner - jnp.mean(inner, axis=-1, keepdims=True)
    result = scaled * (centred - normal * jnp.mean(inner * normal, axis=-1, keepdims=True))
    return (result, jnp.sum(upstream * normal, axis=0), jnp.sum(upstream, axis=0))


def gelu_slope(values):
    return (
        0.5 * (1.0 + lax.erf(values * 0.7071067811865476))
        + values * jnp.exp(-0.5 * values * values) * 0.3989422804014327
    )


def split_heads(packed):
    blocks = packed.reshape(packed.shape[0], 3, HEADS, HEAD_DIM)
    return (blocks[:, 0], blocks[:, 1], blocks[:, 2])


def head_scores(queries, key_rows):
    scores = jnp.einsum("qhd,khd->hqk", queries, key_rows, preferred_element_type=jnp.float32)
    seen = jnp.arange(key_rows.shape[0], dtype=jnp.int32) < SEQ
    return jnp.where(seen[None, None, :], scores * 0.125, -1e30)


def attend(packed):
    queries, key_rows, val_rows = split_heads(packed)
    scores = head_scores(queries, key_rows)
    log_total = jax.nn.logsumexp(scores, axis=-1, keepdims=True)
    weights = jnp.exp(scores - log_total).astype(jnp.bfloat16)
    result = jnp.einsum("hqk,khd->qhd", weights, val_rows, preferred_element_type=jnp.float32)
    return (result.astype(jnp.bfloat16).reshape(packed.shape[0], HEADS * HEAD_DIM), log_total)


def attend_back(packed, log_total, upstream):
    queries, key_rows, val_rows = split_heads(packed)
    weights = jnp.exp(head_scores(queries, key_rows) - log_total)
    incoming = upstream.reshape(queries.shape)
    grad_values = jnp.einsum(
        "hqk,qhd->khd", weights.astype(jnp.bfloat16), incoming, preferred_element_type=jnp.float32
    )
    grad_weights = jnp.einsum(
        "qhd,khd->hqk", incoming, val_rows, preferred_element_type=jnp.float32
    )
    inner = jnp.sum(weights * grad_weights, axis=-1, keepdims=True)
    grad_scores = (weights * (grad_weights - inner)).astype(jnp.bfloat16)
    grad_queries = (
        jnp.einsum("hqk,khd->qhd", grad_scores, key_rows, preferred_element_type=jnp.float32)
        * 0.125
    )
    grad_keys = (
        jnp.einsum("hqk,qhd->khd", grad_scores, queries, preferred_element_type=jnp.float32)
        * 0.125
    )
    stacked = jnp.stack([grad_queries, grad_keys, grad_values], axis=1)
    return stacked.astype(jnp.bfloat16).reshape(packed.shape)


def body(
    n,
    tokens,
    ln_gain,
    ln_bias,
    w_qkv,
    w_proj,
    w_router,
    expert_in,
    expert_out,
    image_count,
    expert_ids,
    slot_index,
    cotangent,
):
    count, width = tokens.shape
    rows = round_up(count, 16)
    layers, share = w_qkv.shape[:2]
    experts, units = expert_in.shape[1:3]
    slots = experts * units
    padded = ((0, rows - count), (0, 0))
    live = (jnp.arange(rows, dtype=jnp.int32) // SEQ < image_count[0]).astype(jnp.float32)[:, None]
    kinds = jnp.arange(experts, dtype=jnp.int32)
    hits = (expert_ids[..., None] == kinds) & (slot_index[..., None] >= 0)
    own_mask = jnp.sum(hits.astype(jnp.float32), axis=2)
    own_mask = jnp.pad(own_mask, ((0, 0),) + padded)
    mask_block = jnp.swapaxes(own_mask, 0, 1).reshape(rows, layers * experts)
    mask_block = jnp.pad(mask_block, ((0, 0), (0, LANES - layers * experts)))
    smalls = jnp.concatenate(
        [
            ln_gain.reshape(2 * layers, share),
            ln_bias.reshape(2 * layers, share),
            jnp.swapaxes(w_router, 1, 2).reshape(layers * experts, share),
        ]
    )
    small_rows = smalls.shape[0]
    smalls = jnp.pad(
        smalls,
        ((0, round_up(small_rows, 16) - small_rows), (0, round_up(share, LANES) - share)),
    )
    (qkv_first, proj_first), (small_all, mask_all) = gather_weights(
        n, (w_qkv[0], w_proj[0]), (smalls, mask_block.astype(jnp.bfloat16))
    )
    small_all = jnp.swapaxes(small_all[:, :small_rows, :share], 0, 1).reshape(small_rows, width)
    gains = small_all[: 2 * layers].astype(jnp.float32).reshape(layers, 2, width)
    biases = small_all[2 * layers : 4 * layers].astype(jnp.float32).reshape(layers, 2, width)
    routers = small_all[4 * layers :].reshape(layers, experts, width)
    masks = mask_all.reshape(n * rows, LANES)[:, : layers * experts].astype(jnp.float32)
    masks = masks.reshape(n * rows, layers, experts)
    qkv_all = [qkv_first]
    proj_all = [proj_first]
    for layer_idx in range(1, layers):
        qkv_all.append(lax.all_gather(w_qkv[layer_idx], "shard", axis=0, tiled=True))
        proj_all.append(lax.all_gather(w_proj[layer_idx], "shard", axis=0, tiled=True))
    state = jnp.pad(tokens.astype(jnp.float32), padded)
    saved = []
    for layer_idx in range(layers):
        gain = gains[layer_idx]
        bias = biases[layer_idx]
        first_out, first_normal, first_scaled = norm_forward(state, gain[0], bias[0])
        first_low = first_out.astype(jnp.bfloat16)
        packed = jnp.dot(first_low, qkv_all[layer_idx], preferred_element_type=jnp.float32).astype(
            jnp.bfloat16
        )
        attended, log_total = attend(packed)
        after = state + jnp.dot(attended, proj_all[layer_idx], preferred_element_type=jnp.float32)
        second_out, second_normal, second_scaled = norm_forward(after, gain[1], bias[1])
        second_low = second_out.astype(jnp.bfloat16)
        group_rows = gather_rows(n, second_low).reshape(n * rows, width)
        logits = lax.dot_general(
            group_rows,
            routers[layer_idx],
            (((1,), (1,)), ((), ())),
            preferred_element_type=jnp.float32,
        )
        group_probs = jax.nn.softmax(logits, axis=-1)
        gates = group_probs * masks[:, layer_idx]
        wide_gates = jnp.repeat(gates, units, axis=1, total_repeat_length=slots)
        table_in = expert_in[layer_idx].reshape(slots, width)
        table_out = expert_out[layer_idx].reshape(slots, width)
        before = lax.dot_general(
            group_rows, table_in, (((1,), (1,)), ((), ())), preferred_element_type=jnp.float32
        )
        raw_hidden = jax.nn.gelu(before, approximate=False)
        hidden = raw_hidden.astype(jnp.bfloat16)
        scaled_hidden = (raw_hidden * wide_gates).astype(jnp.bfloat16)
        partial_rows = jnp.dot(scaled_hidden, table_out, preferred_element_type=jnp.float32)
        (combined,) = scatter_rows(
            n, [partial_rows.astype(jnp.bfloat16).reshape(n, rows, width)], 1
        )
        me = lax.axis_index("shard")
        probs = lax.dynamic_slice_in_dim(group_probs, me * rows, rows, axis=0)
        saved.append(
            (
                first_normal,
                first_scaled,
                first_low,
                packed,
                attended,
                log_total,
                second_normal,
                second_scaled,
                second_low,
                probs,
                wide_gates,
                group_rows,
                before,
                hidden,
                scaled_hidden,
                table_in,
                table_out,
            )
        )
        state = after + combined
    mixed = (state * live).astype(jnp.bfloat16)
    grad_state = jnp.pad(cotangent.astype(jnp.float32), padded) * live
    dense_lists = [None] * layers
    expert_lists = [None] * layers
    for layer_idx in reversed(range(layers)):
        (
            first_normal,
            first_scaled,
            first_low,
            packed,
            attended,
            log_total,
            second_normal,
            second_scaled,
            second_low,
            probs,
            wide_gates,
            group_rows,
            before,
            hidden,
            scaled_hidden,
            table_in,
            table_out,
        ) = saved[layer_idx]
        gain = gains[layer_idx]
        group_grad = gather_rows(n, grad_state.astype(jnp.bfloat16)).reshape(n * rows, width)
        ungated = lax.dot_general(
            group_grad, table_out, (((1,), (1,)), ((), ())), preferred_element_type=jnp.float32
        )
        gate_terms = jnp.sum(
            (ungated * hidden.astype(jnp.float32)).reshape(n, rows, experts, units), axis=-1
        )
        gate_terms = jnp.pad(
            jnp.swapaxes(gate_terms, 1, 2),
            ((0, 0), (0, round_up(experts, 8) - experts), (0, round_up(rows, LANES) - rows)),
        )
        grad_before = (ungated * wide_gates * gelu_slope(before)).astype(jnp.bfloat16)
        row_terms = jnp.dot(grad_before, table_in, preferred_element_type=jnp.float32)
        grad_rows, grad_gates = scatter_rows(
            n, [row_terms.astype(jnp.bfloat16).reshape(n, rows, width), gate_terms], 2
        )
        grad_out = lax.dot_general(
            scaled_hidden, group_grad, (((0,), (0,)), ((), ())), preferred_element_type=jnp.float32
        )
        grad_in = lax.dot_general(
            grad_before, group_rows, (((0,), (0,)), ((), ())), preferred_element_type=jnp.float32
        )
        expert_lists[layer_idx] = [
            lax.psum_scatter(term.astype(jnp.bfloat16), "replica", scatter_dimension=0, tiled=True)
            for term in (grad_in, grad_out)
        ]
        grad_probs = grad_gates[:experts, :rows].T * own_mask[layer_idx]
        grad_logits = probs * (grad_probs - jnp.sum(probs * grad_probs, axis=-1, keepdims=True))
        router_wide = routers[layer_idx].astype(jnp.float32)
        grad_router = jnp.dot(second_low.astype(jnp.float32).T, grad_logits, precision=precise)
        grad_second = grad_rows + jnp.dot(grad_logits, router_wide, precision=precise)
        norm_part, gain_second, bias_second = norm_backward(
            grad_second, gain[1], second_normal, second_scaled
        )
        grad_after = grad_state + norm_part
        grad_proj_in = grad_after.astype(jnp.bfloat16)
        grad_proj = jnp.dot(attended.T, grad_proj_in, preferred_element_type=jnp.float32)
        grad_attended = jnp.dot(
            grad_proj_in, proj_all[layer_idx].T, preferred_element_type=jnp.float32
        ).astype(jnp.bfloat16)
        grad_packed = attend_back(packed, log_total, grad_attended)
        grad_qkv = jnp.dot(first_low.T, grad_packed, preferred_element_type=jnp.float32)
        grad_first = jnp.dot(grad_packed, qkv_all[layer_idx].T, preferred_element_type=jnp.float32)
        norm_first, gain_first, bias_first = norm_backward(
            grad_first, gain[0], first_normal, first_scaled
        )
        grad_state = grad_after + norm_first
        vectors = jnp.stack([gain_first, gain_second, bias_first, bias_second], axis=1)
        edge = jnp.concatenate([grad_router, vectors], axis=1)
        edge = jnp.pad(edge, ((0, 0), (0, LANES - edge.shape[1])))
        dense = jnp.concatenate(
            [
                grad_qkv.astype(jnp.bfloat16),
                grad_proj.astype(jnp.bfloat16),
                edge.astype(jnp.bfloat16),
            ],
            axis=1,
        )
        dense = lax.psum_scatter(dense, "shard", scatter_dimension=0, tiled=True)
        dense_lists[layer_idx] = lax.psum(dense, "replica").astype(jnp.float32)
    expert_grads = []
    for which in range(2):
        expert_grads.append(
            jnp.stack(
                [
                    lax.all_gather(item[which], "replica", axis=0, tiled=True)
                    .astype(jnp.float32)
                    .reshape(experts, units, width)
                    for item in expert_lists
                ]
            )
        )
    dense = jnp.stack(dense_lists)
    packed_width = w_qkv.shape[2]
    start = packed_width + width
    edges = dense[:, :, start : start + experts + 4]
    vectors = jnp.swapaxes(edges[:, :, experts:], 1, 2)
    return (
        mixed[:count],
        grad_state[:count],
        vectors[:, 0:2],
        vectors[:, 2],
        vectors[:, 3],
        dense[:, :, :packed_width],
        dense[:, :, packed_width:start],
        edges[:, :, :experts],
        expert_grads[0],
        expert_grads[1],
    )


def solution(mesh):
    placed = (
        P(("shard", "replica"), None),
        P(None, None, "shard"),
        P(None, None, "shard"),
        P(None, "shard", None),
        P(None, "shard", None),
        P(None, "shard", None),
        P(None, None, "shard", None),
        P(None, None, "shard", None),
        P(("shard", "replica")),
        P(None, ("shard", "replica"), None),
        P(None, ("shard", "replica"), None),
        P(("shard", "replica"), None),
    )
    return jax.shard_map(
        functools.partial(body, mesh.shape["shard"]),
        mesh=mesh,
        in_specs=placed,
        out_specs=(
            P(("shard", "replica"), None),
            P(("shard", "replica"), None),
            P(None, None, "shard"),
            P(None, "shard"),
            P(None, "shard"),
            P(None, "shard", None),
            P(None, "shard", None),
            P(None, "shard", None),
            P(None, None, "shard", None),
            P(None, None, "shard", None),
        ),
        check_vma=False,
    )
```

```python
import functools

import jax
import jax.numpy as jnp
from jax import lax
from jax.experimental import pallas as pl
from jax.experimental.pallas import tpu as pltpu
from jax.sharding import PartitionSpec as P

HEADS = 12
HEAD_DIM = 64
SEQ = 197
LANES = 128
MESH = pl.DeviceIdType.MESH

precise = lax.Precision.HIGHEST
VMEM = pl.BlockSpec(memory_space=pltpu.VMEM)


def round_up(value, step):
    return (value + step - 1) // step * step


def greet(devices):
    barrier = pltpu.get_barrier_semaphore()
    for device in devices:
        pl.semaphore_signal(barrier, inc=1, device_id=device, device_id_type=MESH)
    pl.semaphore_wait(barrier, len(devices))


def group_peers(n):
    me = lax.axis_index("shard")
    rep = lax.axis_index("replica")
    return me, [(lax.rem(me + k, n), rep) for k in range(1, n)]


def gather_kernel(n, x_ref, o_ref, send, recv):
    me, peers = group_peers(n)
    greet(peers)
    copies = []
    for k, peer in enumerate(peers):
        copy = pltpu.make_async_remote_copy(
            src_ref=x_ref,
            dst_ref=o_ref.at[me],
            send_sem=send.at[k],
            recv_sem=recv.at[k],
            device_id=peer,
            device_id_type=MESH,
        )
        copy.start()
        copies.append(copy)
    o_ref[me] = x_ref[...]
    for copy in copies:
        copy.wait()


def gather_rows(n, rows):
    return pl.pallas_call(
        functools.partial(gather_kernel, n),
        out_shape=jax.ShapeDtypeStruct((n,) + rows.shape, rows.dtype),
        in_specs=[VMEM],
        out_specs=VMEM,
        scratch_shapes=[pltpu.SemaphoreType.DMA((n - 1,)), pltpu.SemaphoreType.DMA((n - 1,))],
        compiler_params=pltpu.CompilerParams(collective_id=0, has_side_effects=True),
        name="gather_rows",
    )(rows)


def scatter_kernel(n, count, ahead, *refs):
    parts = refs[:count]
    refs = refs[:count] + refs[count + ahead :]
    outs = refs[count : 2 * count]
    lands = refs[2 * count : 3 * count]
    send, recv = refs[3 * count :]
    me, peers = group_peers(n)
    greet(peers)
    copies = []
    for k, peer in enumerate(peers):
        for i in range(count):
            copy = pltpu.make_async_remote_copy(
                src_ref=parts[i].at[peer[0]],
                dst_ref=lands[i].at[k],
                send_sem=send.at[i, k],
                recv_sem=recv.at[i, k],
                device_id=peer,
                device_id_type=MESH,
            )
            copy.start()
            copies.append(copy)
    for copy in copies:
        copy.wait()
    for i in range(count):
        total = parts[i][me].astype(jnp.float32)
        for k in range(n - 1):
            total = total + lands[i][k].astype(jnp.float32)
        outs[i][...] = total


def scatter_rows(n, parts, call_id, ahead=()):
    count = len(parts)
    return pl.pallas_call(
        functools.partial(scatter_kernel, n, count, len(ahead)),
        out_shape=[jax.ShapeDtypeStruct(part.shape[1:], jnp.float32) for part in parts],
        in_specs=[VMEM] * count + [pl.BlockSpec(memory_space=pl.ANY)] * len(ahead),
        out_specs=[VMEM] * count,
        scratch_shapes=[pltpu.VMEM((n - 1,) + part.shape[1:], part.dtype) for part in parts]
        + [pltpu.SemaphoreType.DMA((count, n - 1)), pltpu.SemaphoreType.DMA((count, n - 1))],
        compiler_params=pltpu.CompilerParams(collective_id=call_id, has_side_effects=True),
        name="scatter_rows",
    )(*parts, *ahead)


def weights_kernel(n, halved, whole, *refs):
    count = halved + whole
    ins = refs[:count]
    outs = refs[count : 2 * count]
    send, recv, pass_send, pass_recv = refs[2 * count :]
    me, peers = group_peers(n)
    rep = lax.axis_index("replica")
    core = lax.rem(rep, 2)
    sibling = (me, rep + 1 - 2 * core)
    greet(peers + [sibling])
    copies = [[] for _ in range(count)]
    for i in list(range(halved, count)) + list(range(halved)):
        for k, peer in enumerate(peers):
            if i < halved:
                source, target = ins[i].at[core], outs[i].at[me, core]
            else:
                source, target = ins[i], outs[i].at[me]
            copy = pltpu.make_async_remote_copy(
                src_ref=source,
                dst_ref=target,
                send_sem=send.at[i, k],
                recv_sem=recv.at[i, k],
                device_id=peer,
                device_id_type=MESH,
            )
            copy.start()
            copies[i].append(copy)
    for i in range(count):
        outs[i][me] = ins[i][...]
    passed = []
    for i in range(halved):
        for k in range(n - 1):
            copies[i][k].wait_recv()
            owner = lax.rem(me + n - 1 - k, n)
            copy = pltpu.make_async_remote_copy(
                src_ref=outs[i].at[owner, core],
                dst_ref=outs[i].at[owner, core],
                send_sem=pass_send.at[i, k],
                recv_sem=pass_recv.at[i, k],
                device_id=sibling,
                device_id_type=MESH,
            )
            copy.start()
            passed.append(copy)
    for i in range(halved, count):
        for copy in copies[i]:
            copy.wait_recv()
    for i in range(count):
        for copy in copies[i]:
            copy.wait_send()
    for copy in passed:
        copy.wait()


def gather_weights(n, halved, whole):
    arrays = [a.reshape(2, a.shape[0] // 2, a.shape[1]) for a in halved] + list(whole)
    count = len(arrays)
    outs = pl.pallas_call(
        functools.partial(weights_kernel, n, len(halved), len(whole)),
        out_shape=[jax.ShapeDtypeStruct((n,) + a.shape, a.dtype) for a in arrays],
        in_specs=[VMEM] * count,
        out_specs=[VMEM] * count,
        scratch_shapes=[
            pltpu.SemaphoreType.DMA((count, n - 1)),
            pltpu.SemaphoreType.DMA((count, n - 1)),
            pltpu.SemaphoreType.DMA((len(halved), n - 1)),
            pltpu.SemaphoreType.DMA((len(halved), n - 1)),
        ],
        compiler_params=pltpu.CompilerParams(collective_id=3, has_side_effects=True),
        name="gather_weights",
    )(*arrays)
    full = [o.reshape(n * a.shape[0], a.shape[1]) for o, a in zip(outs, halved)]
    return full, outs[len(halved) :]


def norm_forward(values, gain, bias):
    centre = values - jnp.mean(values, axis=-1, keepdims=True)
    spread = jnp.mean(centre * centre, axis=-1, keepdims=True)
    scaled = lax.rsqrt(spread + 1e-06)
    normal = centre * scaled
    return (normal * gain + bias, normal, scaled)


def norm_backward(upstream, gain, normal, scaled):
    inner = upstream * gain
    centred = inner - jnp.mean(inner, axis=-1, keepdims=True)
    result = scaled * (centred - normal * jnp.mean(inner * normal, axis=-1, keepdims=True))
    return (result, jnp.sum(upstream * normal, axis=0), jnp.sum(upstream, axis=0))


def split_heads(packed):
    blocks = packed.reshape(packed.shape[0], 3, HEADS, HEAD_DIM)
    return (blocks[:, 0], blocks[:, 1], blocks[:, 2])


def head_scores(queries, key_rows):
    scores = jnp.einsum("qhd,khd->hqk", queries, key_rows, preferred_element_type=jnp.float32)
    seen = jnp.arange(key_rows.shape[0], dtype=jnp.int32) < SEQ
    return jnp.where(seen[None, None, :], scores * 0.125, -1e30)


def attend(packed):
    queries, key_rows, val_rows = split_heads(packed)
    scores = head_scores(queries, key_rows)
    log_total = jax.nn.logsumexp(scores, axis=-1, keepdims=True)
    weights = jnp.exp(scores - log_total).astype(jnp.bfloat16)
    result = jnp.einsum("hqk,khd->qhd", weights, val_rows, preferred_element_type=jnp.float32)
    return (result.astype(jnp.bfloat16).reshape(packed.shape[0], HEADS * HEAD_DIM), log_total)


def attend_back(packed, log_total, upstream):
    queries, key_rows, val_rows = split_heads(packed)
    weights = jnp.exp(head_scores(queries, key_rows) - log_total)
    incoming = upstream.reshape(queries.shape)
    grad_values = jnp.einsum(
        "hqk,qhd->khd", weights.astype(jnp.bfloat16), incoming, preferred_element_type=jnp.float32
    )
    grad_weights = jnp.einsum(
        "qhd,khd->hqk", incoming, val_rows, preferred_element_type=jnp.float32
    )
    inner = jnp.sum(weights * grad_weights, axis=-1, keepdims=True)
    grad_scores = (weights * (grad_weights - inner)).astype(jnp.bfloat16)
    grad_queries = (
        jnp.einsum("hqk,khd->qhd", grad_scores, key_rows, preferred_element_type=jnp.float32)
        * 0.125
    )
    grad_keys = (
        jnp.einsum("hqk,qhd->khd", grad_scores, queries, preferred_element_type=jnp.float32)
        * 0.125
    )
    stacked = jnp.stack([grad_queries, grad_keys, grad_values], axis=1)
    return stacked.astype(jnp.bfloat16).reshape(packed.shape)


def body(
    n,
    tokens,
    ln_gain,
    ln_bias,
    w_qkv,
    w_proj,
    w_router,
    expert_in,
    expert_out,
    image_count,
    expert_ids,
    slot_index,
    cotangent,
):
    count, width = tokens.shape
    rows = round_up(count, 16)
    layers, share = w_qkv.shape[:2]
    experts, units = expert_in.shape[1:3]
    padded = ((0, rows - count), (0, 0))
    live = (jnp.arange(rows, dtype=jnp.int32) // SEQ < image_count[0]).astype(jnp.float32)[:, None]
    kinds = jnp.arange(experts, dtype=jnp.int32)
    hits = (expert_ids[..., None] == kinds) & (slot_index[..., None] >= 0)
    own_mask = jnp.sum(hits.astype(jnp.float32), axis=2)
    own_mask = jnp.pad(own_mask, ((0, 0),) + padded)
    mask_block = jnp.pad(own_mask, ((0, 0), (0, 0), (0, LANES - experts)))
    smalls = jnp.concatenate(
        [
            ln_gain.reshape(2 * layers, share),
            ln_bias.reshape(2 * layers, share),
            jnp.swapaxes(w_router, 1, 2).reshape(layers * experts, share),
        ]
    )
    small_rows = smalls.shape[0]
    smalls = jnp.pad(
        smalls,
        ((0, round_up(small_rows, 16) - small_rows), (0, round_up(share, LANES) - share)),
    )
    (qkv_first, proj_first), (small_all, mask_all) = gather_weights(
        n, (w_qkv[0], w_proj[0]), (smalls, mask_block.astype(jnp.bfloat16))
    )
    small_all = jnp.swapaxes(small_all[:, :small_rows, :share], 0, 1).reshape(small_rows, width)
    gains = small_all[: 2 * layers].astype(jnp.float32).reshape(layers, 2, width)
    biases = small_all[2 * layers : 4 * layers].astype(jnp.float32).reshape(layers, 2, width)
    routers = small_all[4 * layers :].reshape(layers, experts, width)
    column = jnp.arange(LANES, dtype=jnp.int32)[None, :]
    router_tables = jnp.pad(routers, ((0, 0), (0, LANES - experts), (0, 0)))
    qkv_all = [qkv_first]
    proj_all = [proj_first]
    for layer_idx in range(1, layers):
        qkv_all.append(lax.all_gather(w_qkv[layer_idx], "shard", axis=0, tiled=True))
        proj_all.append(lax.all_gather(w_proj[layer_idx], "shard", axis=0, tiled=True))
    state = jnp.pad(tokens.astype(jnp.float32), padded)
    saved = []
    for layer_idx in range(layers):
        gain = gains[layer_idx]
        bias = biases[layer_idx]
        first_out, first_normal, first_scaled = norm_forward(state, gain[0], bias[0])
        first_low = first_out.astype(jnp.bfloat16)
        packed = jnp.dot(first_low, qkv_all[layer_idx], preferred_element_type=jnp.float32).astype(
            jnp.bfloat16
        )
        attended, log_total = attend(packed)
        after = state + jnp.dot(attended, proj_all[layer_idx], preferred_element_type=jnp.float32)
        second_out, second_normal, second_scaled = norm_forward(after, gain[1], bias[1])
        second_low = second_out.astype(jnp.bfloat16)
        group_rows = gather_rows(n, second_low).reshape(n * rows, width)
        logits = lax.dot_general(
            group_rows,
            router_tables[layer_idx],
            (((1,), (1,)), ((), ())),
            preferred_element_type=jnp.float32,
        )
        group_probs = jax.nn.softmax(jnp.where(column < experts, logits, -jnp.inf), axis=-1)
        gates = group_probs * mask_all[:, layer_idx].reshape(n * rows, LANES).astype(jnp.float32)
        kept = []
        partial_rows = None
        for e in range(experts):
            table_in = expert_in[layer_idx, e]
            table_out = expert_out[layer_idx, e]
            before = lax.dot_general(
                group_rows, table_in, (((1,), (1,)), ((), ())), preferred_element_type=jnp.float32
            )
            share_below = 0.5 * (1.0 + lax.erf(before * 0.7071067811865476))
            raw_hidden = before * share_below
            bell = jnp.exp(-0.5 * before * before) * 0.3989422804014327
            slope = (share_below + before * bell).astype(jnp.bfloat16)
            hidden = raw_hidden.astype(jnp.bfloat16)
            scaled_hidden = (raw_hidden * gates[:, e : e + 1]).astype(jnp.bfloat16)
            hidden, scaled_hidden, slope = lax.optimization_barrier((hidden, scaled_hidden, slope))
            kept.append((hidden, scaled_hidden, slope, table_in, table_out))
            term = jnp.dot(scaled_hidden, table_out, preferred_element_type=jnp.float32)
            partial_rows = term if partial_rows is None else partial_rows + term
        (combined,) = scatter_rows(
            n, [partial_rows.astype(jnp.bfloat16).reshape(n, rows, width)], 1
        )
        me = lax.axis_index("shard")
        probs = lax.dynamic_slice_in_dim(group_probs, me * rows, rows, axis=0)[:, :experts]
        saved.append(
            (
                first_normal,
                first_scaled,
                first_low,
                packed,
                attended,
                log_total,
                second_normal,
                second_scaled,
                second_low,
                probs,
                gates,
                group_rows,
                kept,
            )
        )
        state = after + combined
    mixed = (state * live).astype(jnp.bfloat16)
    grad_state = jnp.pad(cotangent.astype(jnp.float32), padded) * live
    dense_lists = [None] * layers
    expert_lists = [None] * layers
    for layer_idx in reversed(range(layers)):
        (
            first_normal,
            first_scaled,
            first_low,
            packed,
            attended,
            log_total,
            second_normal,
            second_scaled,
            second_low,
            probs,
            gates,
            group_rows,
            kept,
        ) = saved[layer_idx]
        gain = gains[layer_idx]
        group_grad = gather_rows(n, grad_state.astype(jnp.bfloat16)).reshape(n * rows, width)
        gate_terms = jnp.zeros((n * rows, LANES), jnp.float32)
        row_terms = None
        pairs = []
        for e in range(experts):
            hidden, scaled_hidden, slope, table_in, table_out = kept[e]
            ungated = lax.dot_general(
                group_grad, table_out, (((1,), (1,)), ((), ())), preferred_element_type=jnp.float32
            )
            agreed = jnp.sum(ungated * hidden.astype(jnp.float32), axis=-1, keepdims=True)
            coarse = lax.reduce_precision(agreed, 8, 7)
            gate_terms = jnp.where(column == e, coarse, gate_terms)
            gate_terms = jnp.where(column == experts + e, agreed - coarse, gate_terms)
            grad_before = (ungated * gates[:, e : e + 1] * slope.astype(jnp.float32)).astype(
                jnp.bfloat16
            )
            term = jnp.dot(grad_before, table_in, preferred_element_type=jnp.float32)
            row_terms = term if row_terms is None else row_terms + term
            pairs.append(((grad_before, group_rows), (scaled_hidden, group_grad)))
        sums = [
            jnp.concatenate(
                [
                    lax.dot_general(
                        pair[which][0],
                        pair[which][1],
                        (((0,), (0,)), ((), ())),
                        preferred_element_type=jnp.float32,
                    ).astype(jnp.bfloat16)
                    for pair in pairs
                ]
            )
            for which in range(2)
        ]
        ahead = list(sums)
        if layer_idx + 1 < layers:
            ahead += expert_lists[layer_idx + 1]
        grad_rows, grad_gates = scatter_rows(
            n,
            [
                row_terms.astype(jnp.bfloat16).reshape(n, rows, width),
                gate_terms.astype(jnp.bfloat16).reshape(n, rows, LANES),
            ],
            2 if layer_idx + 1 == layers else 4,
            ahead,
        )
        expert_lists[layer_idx] = [
            lax.psum_scatter(term, "replica", scatter_dimension=0, tiled=True) for term in sums
        ]
        grad_gates = grad_gates[:, :experts] + grad_gates[:, experts : 2 * experts]
        grad_probs = grad_gates * own_mask[layer_idx]
        grad_logits = probs * (grad_probs - jnp.sum(probs * grad_probs, axis=-1, keepdims=True))
        router_wide = routers[layer_idx].astype(jnp.float32)
        grad_router = jnp.dot(second_low.astype(jnp.float32).T, grad_logits, precision=precise)
        grad_second = grad_rows + jnp.dot(grad_logits, router_wide, precision=precise)
        norm_part, gain_second, bias_second = norm_backward(
            grad_second, gain[1], second_normal, second_scaled
        )
        grad_after = grad_state + norm_part
        grad_proj_in = grad_after.astype(jnp.bfloat16)
        grad_proj = jnp.dot(attended.T, grad_proj_in, preferred_element_type=jnp.float32)
        grad_attended = jnp.dot(
            grad_proj_in, proj_all[layer_idx].T, preferred_element_type=jnp.float32
        ).astype(jnp.bfloat16)
        grad_packed = attend_back(packed, log_total, grad_attended)
        grad_qkv = jnp.dot(first_low.T, grad_packed, preferred_element_type=jnp.float32)
        grad_first = jnp.dot(grad_packed, qkv_all[layer_idx].T, preferred_element_type=jnp.float32)
        norm_first, gain_first, bias_first = norm_backward(
            grad_first, gain[0], first_normal, first_scaled
        )
        grad_state = grad_after + norm_first
        vectors = jnp.stack([gain_first, gain_second, bias_first, bias_second], axis=1)
        edge = jnp.concatenate([grad_router, vectors], axis=1)
        edge = jnp.pad(edge, ((0, 0), (0, LANES - edge.shape[1])))
        dense = jnp.concatenate(
            [
                grad_qkv.astype(jnp.bfloat16),
                grad_proj.astype(jnp.bfloat16),
                edge.astype(jnp.bfloat16),
            ],
            axis=1,
        )
        dense = lax.psum_scatter(dense, "shard", scatter_dimension=0, tiled=True)
        dense_lists[layer_idx] = lax.psum(dense, "replica").astype(jnp.float32)
    expert_grads = []
    for which in range(2):
        expert_grads.append(
            jnp.stack(
                [
                    lax.all_gather(item[which], "replica", axis=0, tiled=True)
                    .astype(jnp.float32)
                    .reshape(experts, units, width)
                    for item in expert_lists
                ]
            )
        )
    dense = jnp.stack(dense_lists)
    packed_width = w_qkv.shape[2]
    start = packed_width + width
    edges = dense[:, :, start : start + experts + 4]
    vectors = jnp.swapaxes(edges[:, :, experts:], 1, 2)
    return (
        mixed[:count],
        grad_state[:count],
        vectors[:, 0:2],
        vectors[:, 2],
        vectors[:, 3],
        dense[:, :, :packed_width],
        dense[:, :, packed_width:start],
        edges[:, :, :experts],
        expert_grads[0],
        expert_grads[1],
    )


def solution(mesh):
    placed = (
        P(("shard", "replica"), None),
        P(None, None, "shard"),
        P(None, None, "shard"),
        P(None, "shard", None),
        P(None, "shard", None),
        P(None, "shard", None),
        P(None, None, "shard", None),
        P(None, None, "shard", None),
        P(("shard", "replica")),
        P(None, ("shard", "replica"), None),
        P(None, ("shard", "replica"), None),
        P(("shard", "replica"), None),
    )
    return jax.shard_map(
        functools.partial(body, mesh.shape["shard"]),
        mesh=mesh,
        in_specs=placed,
        out_specs=(
            P(("shard", "replica"), None),
            P(("shard", "replica"), None),
            P(None, None, "shard"),
            P(None, "shard"),
            P(None, "shard"),
            P(None, "shard", None),
            P(None, "shard", None),
            P(None, "shard", None),
            P(None, None, "shard", None),
            P(None, None, "shard", None),
        ),
        check_vma=False,
    )
```

```python
import functools

import jax
import jax.numpy as jnp
from jax import lax
from jax.experimental import pallas as pl
from jax.experimental.pallas import tpu as pltpu
from jax.sharding import PartitionSpec as P

HEADS = 12
HEAD_DIM = 64
SEQ = 197
LANES = 128
MESH = pl.DeviceIdType.MESH

precise = lax.Precision.HIGHEST
VMEM = pl.BlockSpec(memory_space=pltpu.VMEM)


def round_up(value, step):
    return (value + step - 1) // step * step


def greet(devices):
    barrier = pltpu.get_barrier_semaphore()
    for device in devices:
        pl.semaphore_signal(barrier, inc=1, device_id=device, device_id_type=MESH)
    pl.semaphore_wait(barrier, len(devices))


def group_peers(n):
    me = lax.axis_index("shard")
    rep = lax.axis_index("replica")
    return me, [(lax.rem(me + k, n), rep) for k in range(1, n)]


def gather_kernel(n, x_ref, o_ref, send, recv):
    me, peers = group_peers(n)
    greet(peers)
    copies = []
    for k, peer in enumerate(peers):
        copy = pltpu.make_async_remote_copy(
            src_ref=x_ref,
            dst_ref=o_ref.at[me],
            send_sem=send.at[k],
            recv_sem=recv.at[k],
            device_id=peer,
            device_id_type=MESH,
        )
        copy.start()
        copies.append(copy)
    o_ref[me] = x_ref[...]
    for copy in copies:
        copy.wait()


def gather_rows(n, rows):
    return pl.pallas_call(
        functools.partial(gather_kernel, n),
        out_shape=jax.ShapeDtypeStruct((n,) + rows.shape, rows.dtype),
        in_specs=[VMEM],
        out_specs=VMEM,
        scratch_shapes=[pltpu.SemaphoreType.DMA((n - 1,)), pltpu.SemaphoreType.DMA((n - 1,))],
        compiler_params=pltpu.CompilerParams(collective_id=0, has_side_effects=True),
        name="gather_rows",
    )(rows)


def scatter_kernel(n, count, ahead, *refs):
    parts = refs[:count]
    refs = refs[:count] + refs[count + ahead :]
    outs = refs[count : 2 * count]
    lands = refs[2 * count : 3 * count]
    send, recv = refs[3 * count :]
    me, peers = group_peers(n)
    greet(peers)
    copies = []
    for k, peer in enumerate(peers):
        for i in range(count):
            copy = pltpu.make_async_remote_copy(
                src_ref=parts[i].at[peer[0]],
                dst_ref=lands[i].at[k],
                send_sem=send.at[i, k],
                recv_sem=recv.at[i, k],
                device_id=peer,
                device_id_type=MESH,
            )
            copy.start()
            copies.append(copy)
    for copy in copies:
        copy.wait()
    for i in range(count):
        total = parts[i][me].astype(jnp.float32)
        for k in range(n - 1):
            total = total + lands[i][k].astype(jnp.float32)
        outs[i][...] = total


def scatter_rows(n, parts, call_id, ahead=()):
    count = len(parts)
    return pl.pallas_call(
        functools.partial(scatter_kernel, n, count, len(ahead)),
        out_shape=[jax.ShapeDtypeStruct(part.shape[1:], jnp.float32) for part in parts],
        in_specs=[VMEM] * count + [pl.BlockSpec(memory_space=pl.ANY)] * len(ahead),
        out_specs=[VMEM] * count,
        scratch_shapes=[pltpu.VMEM((n - 1,) + part.shape[1:], part.dtype) for part in parts]
        + [pltpu.SemaphoreType.DMA((count, n - 1)), pltpu.SemaphoreType.DMA((count, n - 1))],
        compiler_params=pltpu.CompilerParams(
            collective_id=call_id, has_side_effects=True, vmem_limit_bytes=40 * 1024 * 1024
        ),
        name="scatter_rows",
    )(*parts, *ahead)


def weights_kernel(n, halved, whole, *refs):
    count = halved + whole
    ins = refs[:count]
    outs = refs[count : 2 * count]
    send, recv, pass_send, pass_recv = refs[2 * count :]
    me, peers = group_peers(n)
    rep = lax.axis_index("replica")
    core = lax.rem(rep, 2)
    sibling = (me, rep + 1 - 2 * core)
    greet(peers + [sibling])
    copies = [[] for _ in range(count)]
    for i in list(range(halved, count)) + list(range(halved)):
        for k, peer in enumerate(peers):
            if i < halved:
                source, target = ins[i].at[core], outs[i].at[me, core]
            else:
                source, target = ins[i], outs[i].at[me]
            copy = pltpu.make_async_remote_copy(
                src_ref=source,
                dst_ref=target,
                send_sem=send.at[i, k],
                recv_sem=recv.at[i, k],
                device_id=peer,
                device_id_type=MESH,
            )
            copy.start()
            copies[i].append(copy)
    for i in range(count):
        outs[i][me] = ins[i][...]
    passed = []
    for i in range(halved):
        for k in range(n - 1):
            copies[i][k].wait_recv()
            owner = lax.rem(me + n - 1 - k, n)
            copy = pltpu.make_async_remote_copy(
                src_ref=outs[i].at[owner, core],
                dst_ref=outs[i].at[owner, core],
                send_sem=pass_send.at[i, k],
                recv_sem=pass_recv.at[i, k],
                device_id=sibling,
                device_id_type=MESH,
            )
            copy.start()
            passed.append(copy)
    for i in range(halved, count):
        for copy in copies[i]:
            copy.wait_recv()
    for i in range(count):
        for copy in copies[i]:
            copy.wait_send()
    for copy in passed:
        copy.wait()


def gather_weights(n, halved, whole):
    arrays = [a.reshape(2, a.shape[0] // 2, a.shape[1]) for a in halved] + list(whole)
    count = len(arrays)
    outs = pl.pallas_call(
        functools.partial(weights_kernel, n, len(halved), len(whole)),
        out_shape=[jax.ShapeDtypeStruct((n,) + a.shape, a.dtype) for a in arrays],
        in_specs=[VMEM] * count,
        out_specs=[VMEM] * count,
        scratch_shapes=[
            pltpu.SemaphoreType.DMA((count, n - 1)),
            pltpu.SemaphoreType.DMA((count, n - 1)),
            pltpu.SemaphoreType.DMA((len(halved), n - 1)),
            pltpu.SemaphoreType.DMA((len(halved), n - 1)),
        ],
        compiler_params=pltpu.CompilerParams(collective_id=3, has_side_effects=True),
        name="gather_weights",
    )(*arrays)
    full = [o.reshape(n * a.shape[0], a.shape[1]) for o, a in zip(outs, halved)]
    return full, outs[len(halved) :]


def norm_forward(values, gain, bias):
    centre = values - jnp.mean(values, axis=-1, keepdims=True)
    spread = jnp.mean(centre * centre, axis=-1, keepdims=True)
    scaled = lax.rsqrt(spread + 1e-06)
    normal = centre * scaled
    return (normal * gain + bias, normal, scaled)


def norm_backward(upstream, gain, normal, scaled):
    inner = upstream * gain
    centred = inner - jnp.mean(inner, axis=-1, keepdims=True)
    result = scaled * (centred - normal * jnp.mean(inner * normal, axis=-1, keepdims=True))
    return (result, jnp.sum(upstream * normal, axis=0), jnp.sum(upstream, axis=0))


def split_heads(packed):
    blocks = packed.reshape(packed.shape[0], 3, HEADS, HEAD_DIM)
    return (blocks[:, 0], blocks[:, 1], blocks[:, 2])


def head_scores(queries, key_rows):
    scores = jnp.einsum("qhd,khd->hqk", queries, key_rows, preferred_element_type=jnp.float32)
    seen = jnp.arange(key_rows.shape[0], dtype=jnp.int32) < SEQ
    return jnp.where(seen[None, None, :], scores * 0.125, -1e30)


def attend(packed):
    queries, key_rows, val_rows = split_heads(packed)
    scores = head_scores(queries, key_rows)
    log_total = jax.nn.logsumexp(scores, axis=-1, keepdims=True)
    weights = jnp.exp(scores - log_total).astype(jnp.bfloat16)
    result = jnp.einsum("hqk,khd->qhd", weights, val_rows, preferred_element_type=jnp.float32)
    return (result.astype(jnp.bfloat16).reshape(packed.shape[0], HEADS * HEAD_DIM), log_total)


def attend_back(packed, log_total, upstream):
    queries, key_rows, val_rows = split_heads(packed)
    weights = jnp.exp(head_scores(queries, key_rows) - log_total)
    incoming = upstream.reshape(queries.shape)
    grad_values = jnp.einsum(
        "hqk,qhd->khd", weights.astype(jnp.bfloat16), incoming, preferred_element_type=jnp.float32
    )
    grad_weights = jnp.einsum(
        "qhd,khd->hqk", incoming, val_rows, preferred_element_type=jnp.float32
    )
    inner = jnp.sum(weights * grad_weights, axis=-1, keepdims=True)
    grad_scores = (weights * (grad_weights - inner)).astype(jnp.bfloat16)
    grad_queries = (
        jnp.einsum("hqk,khd->qhd", grad_scores, key_rows, preferred_element_type=jnp.float32)
        * 0.125
    )
    grad_keys = (
        jnp.einsum("hqk,qhd->khd", grad_scores, queries, preferred_element_type=jnp.float32)
        * 0.125
    )
    stacked = jnp.stack([grad_queries, grad_keys, grad_values], axis=1)
    return stacked.astype(jnp.bfloat16).reshape(packed.shape)


def body(
    n,
    tokens,
    ln_gain,
    ln_bias,
    w_qkv,
    w_proj,
    w_router,
    expert_in,
    expert_out,
    image_count,
    expert_ids,
    slot_index,
    cotangent,
):
    count, width = tokens.shape
    rows = round_up(count, 16)
    layers, share = w_qkv.shape[:2]
    experts, units = expert_in.shape[1:3]
    padded = ((0, rows - count), (0, 0))
    live = (jnp.arange(rows, dtype=jnp.int32) // SEQ < image_count[0]).astype(jnp.float32)[:, None]
    kinds = jnp.arange(experts, dtype=jnp.int32)
    hits = (expert_ids[..., None] == kinds) & (slot_index[..., None] >= 0)
    own_mask = jnp.sum(hits.astype(jnp.float32), axis=2)
    own_mask = jnp.pad(own_mask, ((0, 0),) + padded)
    mask_block = jnp.pad(own_mask, ((0, 0), (0, 0), (0, LANES - experts)))
    smalls = jnp.concatenate(
        [
            ln_gain.reshape(2 * layers, share),
            ln_bias.reshape(2 * layers, share),
            jnp.swapaxes(w_router, 1, 2).reshape(layers * experts, share),
        ]
    )
    small_rows = smalls.shape[0]
    smalls = jnp.pad(
        smalls,
        ((0, round_up(small_rows, 16) - small_rows), (0, round_up(share, LANES) - share)),
    )
    (qkv_first, proj_first), (small_all, mask_all) = gather_weights(
        n, (w_qkv[0], w_proj[0]), (smalls, mask_block.astype(jnp.bfloat16))
    )
    small_all = jnp.swapaxes(small_all[:, :small_rows, :share], 0, 1).reshape(small_rows, width)
    gains = small_all[: 2 * layers].astype(jnp.float32).reshape(layers, 2, width)
    biases = small_all[2 * layers : 4 * layers].astype(jnp.float32).reshape(layers, 2, width)
    routers = small_all[4 * layers :].reshape(layers, experts, width)
    column = jnp.arange(LANES, dtype=jnp.int32)[None, :]
    router_tables = jnp.pad(routers, ((0, 0), (0, LANES - experts), (0, 0)))
    qkv_all = [qkv_first]
    proj_all = [proj_first]
    for layer_idx in range(1, layers):
        qkv_all.append(lax.all_gather(w_qkv[layer_idx], "shard", axis=0, tiled=True))
        proj_all.append(lax.all_gather(w_proj[layer_idx], "shard", axis=0, tiled=True))
    state = jnp.pad(tokens.astype(jnp.float32), padded)
    saved = []
    for layer_idx in range(layers):
        gain = gains[layer_idx]
        bias = biases[layer_idx]
        first_out, first_normal, first_scaled = norm_forward(state, gain[0], bias[0])
        first_low = first_out.astype(jnp.bfloat16)
        packed = jnp.dot(first_low, qkv_all[layer_idx], preferred_element_type=jnp.float32).astype(
            jnp.bfloat16
        )
        attended, log_total = attend(packed)
        after = state + jnp.dot(attended, proj_all[layer_idx], preferred_element_type=jnp.float32)
        second_out, second_normal, second_scaled = norm_forward(after, gain[1], bias[1])
        second_low = second_out.astype(jnp.bfloat16)
        group_rows = gather_rows(n, second_low).reshape(n * rows, width)
        logits = lax.dot_general(
            group_rows,
            router_tables[layer_idx],
            (((1,), (1,)), ((), ())),
            preferred_element_type=jnp.float32,
        )
        group_probs = jax.nn.softmax(jnp.where(column < experts, logits, -jnp.inf), axis=-1)
        gates = group_probs * mask_all[:, layer_idx].reshape(n * rows, LANES).astype(jnp.float32)
        kept = []
        partial_rows = None
        for e in range(experts):
            table_in = expert_in[layer_idx, e]
            table_out = expert_out[layer_idx, e]
            before = lax.dot_general(
                group_rows, table_in, (((1,), (1,)), ((), ())), preferred_element_type=jnp.float32
            )
            share_below = 0.5 * (1.0 + lax.erf(before * 0.7071067811865476))
            raw_hidden = before * share_below
            bell = jnp.exp(-0.5 * before * before) * 0.3989422804014327
            slope = (share_below + before * bell).astype(jnp.bfloat16)
            hidden = raw_hidden.astype(jnp.bfloat16)
            scaled_hidden = (raw_hidden * gates[:, e : e + 1]).astype(jnp.bfloat16)
            hidden, scaled_hidden, slope = lax.optimization_barrier((hidden, scaled_hidden, slope))
            kept.append((hidden, scaled_hidden, slope, table_in, table_out))
            term = jnp.dot(scaled_hidden, table_out, preferred_element_type=jnp.float32)
            partial_rows = term if partial_rows is None else partial_rows + term
        (combined,) = scatter_rows(
            n, [partial_rows.astype(jnp.bfloat16).reshape(n, rows, width)], 1
        )
        me = lax.axis_index("shard")
        probs = lax.dynamic_slice_in_dim(group_probs, me * rows, rows, axis=0)[:, :experts]
        saved.append(
            (
                first_normal,
                first_scaled,
                first_low,
                packed,
                attended,
                log_total,
                second_normal,
                second_scaled,
                second_low,
                probs,
                gates,
                group_rows,
                kept,
            )
        )
        state = after + combined
    mixed = (state * live).astype(jnp.bfloat16)
    grad_state = jnp.pad(cotangent.astype(jnp.float32), padded) * live
    dense_lists = [None] * layers
    expert_lists = [None] * layers
    for layer_idx in reversed(range(layers)):
        (
            first_normal,
            first_scaled,
            first_low,
            packed,
            attended,
            log_total,
            second_normal,
            second_scaled,
            second_low,
            probs,
            gates,
            group_rows,
            kept,
        ) = saved[layer_idx]
        gain = gains[layer_idx]
        group_grad = gather_rows(n, grad_state.astype(jnp.bfloat16)).reshape(n * rows, width)
        gate_terms = jnp.zeros((n * rows, LANES), jnp.float32)
        row_terms = None
        pairs = []
        for e in range(experts):
            hidden, scaled_hidden, slope, table_in, table_out = kept[e]
            ungated = lax.dot_general(
                group_grad, table_out, (((1,), (1,)), ((), ())), preferred_element_type=jnp.float32
            )
            agreed = jnp.sum(ungated * hidden.astype(jnp.float32), axis=-1, keepdims=True)
            coarse = lax.reduce_precision(agreed, 8, 7)
            gate_terms = jnp.where(column == e, coarse, gate_terms)
            gate_terms = jnp.where(column == experts + e, agreed - coarse, gate_terms)
            grad_before = (ungated * gates[:, e : e + 1] * slope.astype(jnp.float32)).astype(
                jnp.bfloat16
            )
            term = jnp.dot(grad_before, table_in, preferred_element_type=jnp.float32)
            row_terms = term if row_terms is None else row_terms + term
            pairs.append(((grad_before, group_rows), (scaled_hidden, group_grad)))
        sums = [
            jnp.concatenate(
                [
                    lax.dot_general(
                        pair[which][0],
                        pair[which][1],
                        (((0,), (0,)), ((), ())),
                        preferred_element_type=jnp.float32,
                    ).astype(jnp.bfloat16)
                    for pair in pairs
                ]
            )
            for which in range(2)
        ]
        ahead = list(sums)
        if layer_idx + 1 < layers:
            ahead += expert_lists[layer_idx + 1]
        grad_rows, grad_gates = scatter_rows(
            n,
            [
                row_terms.astype(jnp.bfloat16).reshape(n, rows, width),
                gate_terms.astype(jnp.bfloat16).reshape(n, rows, LANES),
            ],
            2 if layer_idx + 1 == layers else 4,
            ahead,
        )
        expert_lists[layer_idx] = [
            lax.psum_scatter(term, "replica", scatter_dimension=0, tiled=True) for term in sums
        ]
        grad_gates = grad_gates[:, :experts] + grad_gates[:, experts : 2 * experts]
        grad_probs = grad_gates * own_mask[layer_idx]
        grad_logits = probs * (grad_probs - jnp.sum(probs * grad_probs, axis=-1, keepdims=True))
        router_wide = routers[layer_idx].astype(jnp.float32)
        grad_router = jnp.dot(second_low.astype(jnp.float32).T, grad_logits, precision=precise)
        grad_second = grad_rows + jnp.dot(grad_logits, router_wide, precision=precise)
        norm_part, gain_second, bias_second = norm_backward(
            grad_second, gain[1], second_normal, second_scaled
        )
        grad_after = grad_state + norm_part
        grad_proj_in = grad_after.astype(jnp.bfloat16)
        grad_proj = jnp.dot(attended.T, grad_proj_in, preferred_element_type=jnp.float32)
        grad_attended = jnp.dot(
            grad_proj_in, proj_all[layer_idx].T, preferred_element_type=jnp.float32
        ).astype(jnp.bfloat16)
        grad_packed = attend_back(packed, log_total, grad_attended)
        grad_qkv = jnp.dot(first_low.T, grad_packed, preferred_element_type=jnp.float32)
        grad_first = jnp.dot(grad_packed, qkv_all[layer_idx].T, preferred_element_type=jnp.float32)
        norm_first, gain_first, bias_first = norm_backward(
            grad_first, gain[0], first_normal, first_scaled
        )
        grad_state = grad_after + norm_first
        vectors = jnp.stack([gain_first, gain_second, bias_first, bias_second], axis=1)
        edge = jnp.concatenate([grad_router, vectors], axis=1)
        edge = jnp.pad(edge, ((0, 0), (0, LANES - edge.shape[1])))
        dense = jnp.concatenate(
            [
                grad_qkv.astype(jnp.bfloat16),
                grad_proj.astype(jnp.bfloat16),
                edge.astype(jnp.bfloat16),
            ],
            axis=1,
        )
        (dense,) = scatter_rows(n, [dense.reshape(n, share, dense.shape[1])], 5)
        dense = dense.astype(jnp.bfloat16)
        dense_lists[layer_idx] = lax.psum(dense, "replica").astype(jnp.float32)
    expert_grads = []
    for which in range(2):
        expert_grads.append(
            jnp.stack(
                [
                    lax.all_gather(item[which], "replica", axis=0, tiled=True)
                    .astype(jnp.float32)
                    .reshape(experts, units, width)
                    for item in expert_lists
                ]
            )
        )
    dense = jnp.stack(dense_lists)
    packed_width = w_qkv.shape[2]
    start = packed_width + width
    edges = dense[:, :, start : start + experts + 4]
    vectors = jnp.swapaxes(edges[:, :, experts:], 1, 2)
    return (
        mixed[:count],
        grad_state[:count],
        vectors[:, 0:2],
        vectors[:, 2],
        vectors[:, 3],
        dense[:, :, :packed_width],
        dense[:, :, packed_width:start],
        edges[:, :, :experts],
        expert_grads[0],
        expert_grads[1],
    )


def solution(mesh):
    placed = (
        P(("shard", "replica"), None),
        P(None, None, "shard"),
        P(None, None, "shard"),
        P(None, "shard", None),
        P(None, "shard", None),
        P(None, "shard", None),
        P(None, None, "shard", None),
        P(None, None, "shard", None),
        P(("shard", "replica")),
        P(None, ("shard", "replica"), None),
        P(None, ("shard", "replica"), None),
        P(("shard", "replica"), None),
    )
    return jax.shard_map(
        functools.partial(body, mesh.shape["shard"]),
        mesh=mesh,
        in_specs=placed,
        out_specs=(
            P(("shard", "replica"), None),
            P(("shard", "replica"), None),
            P(None, None, "shard"),
            P(None, "shard"),
            P(None, "shard"),
            P(None, "shard", None),
            P(None, "shard", None),
            P(None, "shard", None),
            P(None, None, "shard", None),
            P(None, None, "shard", None),
        ),
        check_vma=False,
    )
```
